256 devices in a mesh: island: 16 (over y_lo, x, core), fsdp: 16 (over z, y_hi).
Axes of the slice: x: 4, y: 4 (y_hi: 2, y_lo: 2; y = y_hi * 2 + y_lo), z: 8, core: 2. Of those that a mesh axis runs over, the one named last changes fastest.
Arguments:
- tokens: bfloat16 [16, 4096, 8192], P('island', 'fsdp'), may hold values from -6 to 6
- cotangent: bfloat16 [16, 4096, 1024], P('island', 'fsdp'), may hold values from -0.09375 to 0.09375
- params: float32 [16, 8192, 1024], P('island', 'fsdp'), may hold values from -0.18 to 0.18
- first_moment: bfloat16 [16, 8192, 1024], P('island', 'fsdp'), may hold values from -3 to 3
- second_moment: bfloat16 [16, 8192, 1024], P('island', 'fsdp'), may hold values from 0.25 to 4
- base: float32 [8192, 512], P(('fsdp', 'island')), may hold values from -0.18 to 0.18
- outer_momentum: float32 [8192, 512], P(('fsdp', 'island')), may hold values from -0.06 to 0.06
- head_order: int32 [8], replicated, may hold values from 0 to 7, each once
- step_fragment: int32 [1], replicated, may hold values from 0 to 1
Outputs:
- params_out: float32 [16, 8192, 1024], P('island', 'fsdp')
- first_out: bfloat16 [16, 8192, 1024], P('island', 'fsdp')
- second_out: bfloat16 [16, 8192, 1024], P('island', 'fsdp')
- base_out: float32 [8192, 512], P(('fsdp', 'island'))
- momentum_out: float32 [8192, 512], P(('fsdp', 'island'))
The draws below stay inside these ranges and needn't reach their ends.
All inputs are finite; a program needn't handle non-finite values.
Results may differ from the reference program's by a relative error of at most 0.012.
Values may be sent and summed in bfloat16 or wider, within the bound.
A program may use at most 128 MiB of HBM per device.

```python
import math
import jax
import jax.numpy as jnp
from jax import lax

D = 8192
KVH = 8
HD = 128
SYNC = 4
TOK_DEV = 256
KV = 1024
FC = 512
FRAGS = 2
TOKENS = 4096
N_ISLAND = 16
N_FSDP = 16


def with_spikes(drawn, rng, source, target, parts, factor):
    owner, partner = [(jnp.arange(drawn.shape[position]) // (drawn.shape[position] // parts)).reshape([-1 if axis == position else 1 for axis in range(drawn.ndim)]) for position in (source, target)]
    chosen = jax.random.permutation(rng, parts)[partner]
    strong = (owner == chosen) | (owner == (partner + parts // 2) % parts)
    return jnp.where(strong, factor * drawn, drawn)


def block_scale(own_key, extent, split, low, largest):
    gain, own = 1.0, jax.random.fold_in(own_key, 6)
    for dim, blocks in split:
        draws = jnp.exp(jax.random.uniform(jax.random.fold_in(own, dim), (blocks,), jnp.float32, low / len(split), largest / len(split)))
        gain = gain * jnp.repeat(draws, extent[dim] // blocks).reshape([-1 if axis == dim else 1 for axis in range(len(extent))])
    return gain


def centred(key, extent, spread, bound, cuts=(), kind=jnp.bfloat16):
    loudness = block_scale(key, extent, cuts, -0.22, 0.18) if cuts else 1.0
    entries = jax.random.normal(key, extent, jnp.float32) * spread * loudness
    return jnp.minimum(jnp.maximum(entries, -bound), bound).astype(kind)


def bell_draw_with(stream_key, shape, spread, limit, split, heavy, kind=jnp.bfloat16):
    entries = spread * jax.random.normal(stream_key, shape, jnp.float32)
    if split:
        entries = entries * block_scale(stream_key, shape, split, -0.22, 0.18)
    return jnp.clip(with_spikes(entries, jax.random.fold_in(stream_key, 3), *heavy), -limit, limit).astype(kind)


def setup_inputs(seed: int = 0) -> dict:
    arg_keys = jax.random.split(jax.random.key(seed), 10)
    return {
        "tokens": bell_draw_with(arg_keys[0], (N_ISLAND, TOKENS, D), 1.0, 6.0, ((0, 16), (1, 16)), (1, 2, 16, 2.0)),
        "cotangent": centred(arg_keys[1], (N_ISLAND, TOKENS, KV), (TOKENS ** -0.5), 0.09375, ((0, 16), (1, 16))),
        "params": centred(arg_keys[2], (N_ISLAND, D, KV), 0.03, 0.18, ((0, 16), (1, 16)), jnp.float32),
        "first_moment": centred(arg_keys[3], (N_ISLAND, D, KV), 0.5, 3.0, ((0, 16), (1, 16))),
        "second_moment": jnp.clip(jnp.exp(math.log(4.0) - 2.7725887 * jax.random.uniform(arg_keys[4], (N_ISLAND, D, KV), jnp.float32) ** block_scale(arg_keys[4], (N_ISLAND, D, KV), ((0, 16), (1, 16)), -0.2, 0.2)), 0.25, 4.0).astype(jnp.bfloat16),
        "base": centred(arg_keys[5], (D, FC), 0.03, 0.18, ((0, 256),), jnp.float32),
        "outer_momentum": centred(arg_keys[6], (D, FC), 0.01, 0.06, ((0, 256),), jnp.float32),
        "head_order": jax.random.permutation(arg_keys[7], KVH).astype(jnp.int32),
        "step_fragment": jax.random.randint(arg_keys[8], (1,), 0, FRAGS).astype(jnp.int32),
    }


def inner_step(tokens, cotangent, params, first_moment, second_moment):
    token_blocks = tokens.reshape(N_FSDP, TOK_DEV, D)
    grad_blocks = cotangent.reshape(N_FSDP, TOK_DEV, KV)

    def add_block(total, pair):
        xs, ds = pair
        part = jnp.dot(xs.T, ds, preferred_element_type=jnp.float32)
        part = lax.optimization_barrier(part.astype(jnp.bfloat16)).astype(jnp.float32)
        return (total + part, None)
    grad, _ = lax.scan(add_block, jnp.zeros((D, KV), jnp.float32), (token_blocks, grad_blocks))
    moment_one = 0.9 * first_moment.astype(jnp.float32) + 0.1 * grad
    moment_two = 0.95 * second_moment.astype(jnp.float32) + 0.05 * grad * grad
    stepped = params - 0.01 * (moment_one / (jnp.sqrt(moment_two) + 1e-08) + 0.1 * params)
    return (stepped, moment_one.astype(jnp.bfloat16), moment_two.astype(jnp.bfloat16))

def reference(tokens, cotangent, params, first_moment, second_moment, base, outer_momentum, head_order, step_fragment):
    stepped, first_out, second_out = lax.map(lambda group: inner_step(*group), (tokens, cotangent, params, first_moment, second_moment))
    heads = lax.dynamic_slice(head_order, (step_fragment[0] * SYNC,), (SYNC,))
    shaped = stepped.reshape(N_ISLAND, D, KVH, HD)
    fragment = jnp.take(shaped, heads, axis=2).reshape(N_ISLAND, D, FC)
    delta = base - lax.optimization_barrier(jnp.sum(fragment, axis=0)) / N_ISLAND
    momentum_out = 0.9 * outer_momentum + delta
    base_out = base - 0.7 * (delta + 0.9 * momentum_out)
    placed = jnp.broadcast_to(base_out.reshape(1, D, SYNC, HD), (N_ISLAND, D, SYNC, HD))
    params_out = shaped.at[:, :, heads, :].set(placed).reshape(N_ISLAND, D, KV)
    return (params_out, first_out, second_out, base_out, momentum_out)
```

```python
import functools

import jax
import jax.numpy as jnp
from jax import lax
from jax.experimental import pallas as pl
from jax.experimental.pallas import tpu as pltpu
from jax.sharding import PartitionSpec as P

KVH = 8
HD = 128
SYNC = 4
Z = 8
HALF = 256
GC = 256
MESH = pl.DeviceIdType.MESH
F32 = jnp.float32
BF16 = jnp.bfloat16


def partial_product(a, b):
    return lax.dot_general(a, b, (((0,), (0,)), ((), ())), preferred_element_type=F32)


def sync_kernel(
    order_ref,
    step_ref,
    tokens,
    cotangent,
    params,
    first_moment,
    second_moment,
    base,
    outer_momentum,
    out_weights,
    out_first,
    out_second,
    out_base,
    out_momentum,
    cot_raw,
    cot,
    tok,
    tok_stage,
    sent,
    got,
    weights_v,
    first_v,
    second_v,
    base_v,
    outer_v,
    weights_p,
    first_p,
    second_p,
    new_weights,
    new_first,
    new_second,
    frag,
    frag_got,
    base_sent,
    base_all,
    base_new,
    outer_new,
    cot_load,
    own_load,
    stage_load,
    state_load,
    y_send_cot,
    y_recv_cot,
    y_send_tok,
    y_recv_tok,
    z_send,
    z_recv,
    frag_send,
    frag_recv,
    base_send,
    base_recv,
    store_sem,
    weights_store,
    small_store,
):
    island = lax.axis_index("island")
    fsdp = lax.axis_index("fsdp")
    islands = lax.axis_size("island")
    z = fsdp // 2
    h = fsdp % 2
    partner = (island, z * 2 + (1 - h))
    up = (island, ((z + 1) % Z) * 2 + h)
    down = (island, ((z + Z - 1) % Z) * 2 + h)
    deltas = (4, 3, 5, 2, 6, 1, 7, 0)
    token_order = (
        (0, 0), (0, 1), (1, 0), (2, 1), (1, 1), (2, 0), (3, 0), (4, 1),
        (3, 1), (4, 0), (5, 0), (6, 1), (5, 1), (6, 0), (7, 0), (7, 1),
    )

    barrier = pltpu.get_barrier_semaphore()
    for peer in (partner, up, down):
        pl.semaphore_signal(barrier, inc=1, device_id=peer, device_id_type=MESH)

    def greet(k, carry):
        pl.semaphore_signal(
            barrier, inc=1, device_id=(lax.rem(island + k, islands), fsdp), device_id_type=MESH
        )
        return carry

    cot_copy = pltpu.make_async_copy(cotangent, cot_raw, cot_load)
    cot_copy.start()

    def own_copy(s, r):
        column = ((z + deltas[s]) % Z * 2 + h) * 2 * HALF + r * HALF
        return pltpu.make_async_copy(
            tokens.at[:, pl.ds(pl.multiple_of(column, HALF), HALF)],
            tok.at[s, r, pl.ds(0, HALF), :],
            own_load.at[s, r],
        )

    def stage_copy(s, r):
        column = ((z + deltas[s]) % Z * 2 + (1 - h)) * 2 * HALF + r * HALF
        return pltpu.make_async_copy(
            tokens.at[:, pl.ds(pl.multiple_of(column, HALF), HALF)],
            tok_stage.at[s, r],
            stage_load.at[s, r],
        )

    def y_cot(g):
        return pltpu.make_async_remote_copy(
            cot.at[g, pl.ds(0, HALF), :],
            cot.at[g, pl.ds(HALF, HALF), :],
            y_send_cot.at[g],
            y_recv_cot.at[g],
            device_id=partner,
            device_id_type=MESH,
        )

    def y_tok(s, r):
        return pltpu.make_async_remote_copy(
            tok_stage.at[s, r],
            tok.at[s, r, pl.ds(HALF, HALF), :],
            y_send_tok.at[s, r],
            y_recv_tok.at[s, r],
            device_id=partner,
            device_id_type=MESH,
        )

    for s, r in token_order:
        stage_copy(s, r).start()
    for s, r in token_order:
        own_copy(s, r).start()
    state = [
        pltpu.make_async_copy(src, dst, state_load.at[i])
        for i, (src, dst) in enumerate(
            (
                (params, weights_v),
                (first_moment, first_v),
                (second_moment, second_v),
                (base, base_v),
                (outer_momentum, outer_v),
            )
        )
    ]
    for copy in state:
        copy.start()
    lax.fori_loop(1, islands, greet, 0)

    first_part = step_ref[0] == 0

    def head_of(j):
        return jnp.where(first_part, order_ref[j], order_ref[lax.rem(j + SYNC, KVH)])

    def columns_of(head, source, rows):
        found = source[rows, 0:HD]
        for other in range(1, KVH):
            found = lax.select(head == other, source[rows, other * HD : (other + 1) * HD], found)
        return found

    cot_copy.wait()
    for j in range(KVH):
        cot[j // 2, 0:HALF, (j % 2) * HD : (j % 2 + 1) * HD] = columns_of(
            head_of(j), cot_raw, slice(0, HALF)
        )

    pl.semaphore_wait(barrier, 3 + islands - 1)

    def send_tok(pairs):
        for s, r in pairs:
            stage_copy(s, r).wait()
            y_tok(s, r).start()

    y_cot(0).start()
    send_tok(token_order[:2])
    y_cot(1).start()
    send_tok(token_order[2:6])
    y_cot(2).start()
    y_cot(3).start()
    send_tok(token_order[6:])

    def z_copy(way, stage, g, r):
        return pltpu.make_async_remote_copy(
            sent.at[way, stage, g, r],
            got.at[way, stage, g, r],
            z_send.at[way, stage, g, r],
            z_recv.at[way, stage, g, r],
            device_id=(up, down)[way],
            device_id_type=MESH,
        )

    def need_tok(s, r):
        own_copy(s, r).wait()
        y_tok(s, r).wait_recv()

    def need_cot(g):
        y_cot(g).wait_recv()

    def term(s, g, r):
        return partial_product(tok[s, r], cot[g])

    def pass_on(way, stage, s, g, r):
        total = term(s, g, r)
        if stage >= 1:
            z_copy(way, stage - 1, g, r).wait_recv()
            total = total + got[way, stage - 1, g, r].astype(F32)
        sent[way, stage, g, r] = total.astype(BF16)
        z_copy(way, stage, g, r).start()

    def ends(g):
        pass_on(0, 0, 0, g, 0)
        pass_on(1, 0, 0, g, 1)

    def third(first_use, low):
        for i in range(2):
            if first_use:
                need_tok(1, i)
                need_tok(2, 1 - i)

            def body(g, carry, i=i):
                for way, s, r in ((0, 1, i), (1, 2, 1 - i)):
                    if i == 0:
                        pass_on(way, 1, s, g, r)
                    else:
                        sent[way, 1, g, r] = term(s, g, r).astype(BF16)
                        z_copy(way, 1, g, r).start()
                return carry

            lax.fori_loop(low, low + 2, body, 0)

    def middle(stage, first_use, low):
        s_up, s_down = 2 * stage - 1, 2 * stage

        for i in range(2):
            if first_use:
                need_tok(s_up, i)
                need_tok(s_down, 1 - i)

            def body(g, carry, i=i):
                pass_on(0, stage, s_up, g, i)
                pass_on(1, stage, s_down, g, 1 - i)
                return carry

            lax.fori_loop(low, low + 2, body, 0)

    def sort_heads(low):
        def body(item, carry):
            j = low + item // 2
            rows = pl.ds(pl.multiple_of(item % 2 * HALF, HALF), HALF)
            head = head_of(j)
            weights_p[j, rows, :] = columns_of(head, weights_v, rows)
            first_p[j, rows, :] = columns_of(head, first_v, rows)
            second_p[j, rows, :] = columns_of(head, second_v, rows)
            return carry

        lax.fori_loop(0, 2 * SYNC, body, 0)

    def own_rows(low, fragment):
        def body(item, carry):
            r = item // 2
            g = low + item % 2
            rows = pl.ds(pl.multiple_of(r * HALF, HALF), HALF)
            grad = term(7, g, r)
            for way in range(2):
                z_copy(way, 3, g, r).wait_recv()
                grad = grad + got[way, 3, g, r].astype(F32)
            for k in range(2):
                j = 2 * g + k
                part = grad[:, k * HD : (k + 1) * HD]
                one = 0.9 * first_p[j, rows, :].astype(F32) + 0.1 * part
                two = 0.95 * second_p[j, rows, :].astype(F32) + 0.05 * part * part
                weights = weights_p[j, rows, :]
                stepped = weights - 0.01 * (one / (jnp.sqrt(two) + 1e-08) + 0.1 * weights)
                new_first[j, rows, :] = one.astype(BF16)
                new_second[j, rows, :] = two.astype(BF16)
                if fragment:
                    frag[rows, pl.ds(pl.multiple_of(j * HD, HD), HD)] = stepped.astype(BF16)
                else:
                    new_weights[j, rows, :] = stepped
            heads = pl.ds(2 * g, 2)
            pltpu.make_async_copy(
                new_first.at[heads, rows, :], out_first.at[heads, rows, :], store_sem.at[0, g, r]
            ).start()
            pltpu.make_async_copy(
                new_second.at[heads, rows, :], out_second.at[heads, rows, :], store_sem.at[1, g, r]
            ).start()
            if not fragment:
                pltpu.make_async_copy(
                    new_weights.at[heads, rows, :],
                    out_weights.at[heads, rows, :],
                    weights_store.at[g, r],
                ).start()
            return carry

        lax.fori_loop(0, 4, body, 0)

    share = base.shape[0]

    def frag_copy(k):
        peer = lax.rem(island + k, islands)
        return pltpu.make_async_remote_copy(
            frag.at[pl.ds(pl.multiple_of(peer * share, share), share), :],
            frag_got.at[k],
            frag_send.at[k],
            frag_recv.at[k],
            device_id=(peer, fsdp),
            device_id_type=MESH,
        )

    def base_copy(k):
        return pltpu.make_async_remote_copy(
            base_sent,
            base_all.at[pl.ds(pl.multiple_of(island * share, share), share), :],
            base_send.at[k],
            base_recv.at[k],
            device_id=(lax.rem(island + k, islands), fsdp),
            device_id_type=MESH,
        )

    def each_peer(action):
        def body(k, carry):
            action(k)
            return carry

        lax.fori_loop(1, islands, body, 0)

    def outer_step():
        mine = pl.ds(pl.multiple_of(island * share, share), share)

        def add(k, total):
            frag_copy(k).wait_recv()
            return total + frag_got[k].astype(F32)

        total = lax.fori_loop(1, islands, add, frag[mine, :].astype(F32))
        delta = base_v[...] - total / islands
        momentum = 0.9 * outer_v[...] + delta
        following = base_v[...] - 0.7 * (delta + 0.9 * momentum)
        base_sent[...] = following.astype(BF16)
        base_all[mine, :] = following.astype(BF16)
        base_new[...] = following
        outer_new[...] = momentum
        each_peer(lambda k: base_copy(k).start())

    need_cot(0)
    need_tok(0, 0)
    pass_on(0, 0, 0, 0, 0)
    need_tok(0, 1)
    pass_on(1, 0, 0, 0, 1)
    need_cot(1)
    ends(1)
    third(True, 0)
    need_cot(2)
    ends(2)
    need_cot(3)
    ends(3)
    third(False, 2)
    for copy in state:
        copy.wait()
    sort_heads(0)
    middle(2, True, 0)
    middle(3, True, 0)
    middle(2, False, 2)
    sort_heads(SYNC)
    need_tok(7, 0)
    need_tok(7, 1)
    own_rows(0, True)
    each_peer(lambda k: frag_copy(k).start())
    middle(3, False, 2)
    outer_step()
    small = [
        pltpu.make_async_copy(base_new, out_base, small_store.at[0]),
        pltpu.make_async_copy(outer_new, out_momentum, small_store.at[1]),
    ]
    for copy in small:
        copy.start()
    own_rows(2, False)
    each_peer(lambda k: base_copy(k).wait_recv())
    for j in range(SYNC):
        new_weights[j] = base_all[:, j * HD : (j + 1) * HD].astype(F32)
    front = pltpu.make_async_copy(
        new_weights.at[pl.ds(0, SYNC)], out_weights.at[pl.ds(0, SYNC)], small_store.at[2]
    )
    front.start()

    for g in range(4):
        y_cot(g).wait_send()
    for s, r in token_order:
        y_tok(s, r).wait_send()
    for way in range(2):
        for g in range(4):
            z_copy(way, 0, g, way).wait_send()

    def sends(item, carry):
        for way in range(2):
            z_copy(way, 1 + item // 8, item // 2 % 4, item % 2).wait_send()
        return carry

    lax.fori_loop(0, 24, sends, 0)
    each_peer(lambda k: frag_copy(k).wait_send())
    each_peer(lambda k: base_copy(k).wait_send())
    for copy in small:
        copy.wait()

    def stores(item, carry):
        g = item // 2
        r = item % 2
        rows = pl.ds(pl.multiple_of(r * HALF, HALF), HALF)
        heads = pl.ds(2 * g, 2)
        pltpu.make_async_copy(
            new_first.at[heads, rows, :], out_first.at[heads, rows, :], store_sem.at[0, g, r]
        ).wait()
        pltpu.make_async_copy(
            new_second.at[heads, rows, :], out_second.at[heads, rows, :], store_sem.at[1, g, r]
        ).wait()
        return carry

    lax.fori_loop(0, 8, stores, 0)

    def weight_stores(item, carry):
        g = 2 + item // 2
        r = item % 2
        rows = pl.ds(pl.multiple_of(r * HALF, HALF), HALF)
        heads = pl.ds(2 * g, 2)
        pltpu.make_async_copy(
            new_weights.at[heads, rows, :], out_weights.at[heads, rows, :], weights_store.at[g, r]
        ).wait()
        return carry

    lax.fori_loop(0, 4, weight_stores, 0)
    front.wait()


def placing_kernel(
    order_ref, step_ref, weights, first, second, base, momentum, w_out, f_out, s_out, b_out, m_out
):
    for head in range(KVH):
        place = 0
        for j in range(1, KVH):
            found = order_ref[lax.rem(step_ref[0] * SYNC + j, KVH)] == head
            place = place + jnp.where(found, j, 0)
        columns = slice(head * HD, (head + 1) * HD)
        w_out[:, columns] = weights[place]
        f_out[:, columns] = first[place]
        s_out[:, columns] = second[place]

    @pl.when(pl.program_id(0) == 0)
    def _():
        b_out[...] = base[...]
        m_out[...] = momentum[...]


def shards(
    tokens,
    cotangent,
    params,
    first_moment,
    second_moment,
    base,
    outer_momentum,
    head_order,
    step_fragment,
):
    rows, width = params.shape[1:]
    share, columns = base.shape
    islands = lax.axis_size("island")
    smem = pl.BlockSpec(memory_space=pltpu.SMEM)
    anywhere = pl.BlockSpec(memory_space=pl.ANY)
    dma = pltpu.SemaphoreType.DMA
    made = pl.pallas_call(
        sync_kernel,
        name="inner_step_and_outer_sync",
        out_shape=(
            jax.ShapeDtypeStruct((KVH, rows, HD), F32),
            jax.ShapeDtypeStruct((KVH, rows, HD), BF16),
            jax.ShapeDtypeStruct((KVH, rows, HD), BF16),
            jax.ShapeDtypeStruct((share, columns), F32),
            jax.ShapeDtypeStruct((share, columns), F32),
        ),
        in_specs=[smem] * 2 + [anywhere] * 7,
        out_specs=(anywhere,) * 5,
        scratch_shapes=[
            pltpu.VMEM((HALF, width), BF16),
            pltpu.VMEM((4, 2 * HALF, GC), BF16),
            pltpu.VMEM((Z, 2, 2 * HALF, HALF), BF16),
            pltpu.VMEM((Z, 2, HALF, HALF), BF16),
            pltpu.VMEM((2, 4, 4, 2, HALF, GC), BF16),
            pltpu.VMEM((2, 4, 4, 2, HALF, GC), BF16),
            pltpu.VMEM((rows, width), F32),
            pltpu.VMEM((rows, width), BF16),
            pltpu.VMEM((rows, width), BF16),
            pltpu.VMEM((share, columns), F32),
            pltpu.VMEM((share, columns), F32),
            pltpu.VMEM((KVH, rows, HD), F32),
            pltpu.VMEM((KVH, rows, HD), BF16),
            pltpu.VMEM((KVH, rows, HD), BF16),
            pltpu.VMEM((KVH, rows, HD), F32),
            pltpu.VMEM((KVH, rows, HD), BF16),
            pltpu.VMEM((KVH, rows, HD), BF16),
            pltpu.VMEM((rows, columns), BF16),
            pltpu.VMEM((16, share, columns), BF16),
            pltpu.VMEM((share, columns), BF16),
            pltpu.VMEM((rows, columns), BF16),
            pltpu.VMEM((share, columns), F32),
            pltpu.VMEM((share, columns), F32),
            dma,
            dma((Z, 2)),
            dma((Z, 2)),
            dma((5,)),
            dma((4,)),
            dma((4,)),
            dma((Z, 2)),
            dma((Z, 2)),
            dma((2, 4, 4, 2)),
            dma((2, 4, 4, 2)),
            dma((16,)),
            dma((16,)),
            dma((16,)),
            dma((16,)),
            dma((2, 4, 2)),
            dma((4, 2)),
            dma((3,)),
        ],
        compiler_params=pltpu.CompilerParams(
            collective_id=0, has_side_effects=True, vmem_limit_bytes=60 * 2**20
        ),
        cost_estimate=pl.CostEstimate(
            flops=2 * 256 * 8192 * 1024, bytes_accessed=13 * 2**20, transcendentals=rows * width
        ),
    )(
        head_order,
        step_fragment,
        tokens[0],
        cotangent[0],
        params[0],
        first_moment[0],
        second_moment[0],
        base,
        outer_momentum,
    )
    steps = 4
    tall = rows // steps
    block = pl.BlockSpec((KVH, tall, HD), lambda i: (0, i, 0))
    wide = pl.BlockSpec((tall, width), lambda i: (i, 0))
    small = pl.BlockSpec((share, columns), lambda i: (0, 0))
    weights, first, second, base_next, momentum_next = pl.pallas_call(
        placing_kernel,
        name="heads_in_place",
        grid=(steps,),
        out_shape=(
            jax.ShapeDtypeStruct((rows, width), F32),
            jax.ShapeDtypeStruct((rows, width), BF16),
            jax.ShapeDtypeStruct((rows, width), BF16),
            jax.ShapeDtypeStruct((share, columns), F32),
            jax.ShapeDtypeStruct((share, columns), F32),
        ),
        in_specs=[smem, smem, block, block, block, small, small],
        out_specs=(wide, wide, wide, small, small),
        compiler_params=pltpu.CompilerParams(vmem_limit_bytes=16 * 2**20),
    )(head_order, step_fragment, *made)
    return (weights[None], first[None], second[None], base_next, momentum_next)


def solution(mesh):
    placed = (
        P("island", "fsdp", None),
        P("island", "fsdp", None),
        P("island", "fsdp", None),
        P("island", "fsdp", None),
        P("island", "fsdp", None),
        P(("fsdp", "island"), None),
        P(("fsdp", "island"), None),
        P(),
        P(),
    )
    return jax.shard_map(
        shards,
        mesh=mesh,
        in_specs=placed,
        out_specs=(
            P("island", "fsdp", None),
            P("island", "fsdp", None),
            P("island", "fsdp", None),
            P(("fsdp", "island"), None),
            P(("fsdp", "island"), None),
        ),
        check_vma=False,
    )
```

```python
import functools

import jax
import jax.numpy as jnp
from jax import lax
from jax.experimental import pallas as pl
from jax.experimental.pallas import tpu as pltpu
from jax.sharding import PartitionSpec as P

KVH = 8
HD = 128
SYNC = 4
Z = 8
HALF = 256
EIGHTH = 128
GC = 256
MESH = pl.DeviceIdType.MESH
F32 = jnp.float32
BF16 = jnp.bfloat16


def partial_product(a, b):
    return lax.dot_general(a, b, (((0,), (0,)), ((), ())), preferred_element_type=F32)


def sync_kernel(
    order,
    step_ref,
    tokens,
    cotangent,
    params,
    first_moment,
    second_moment,
    base,
    outer_momentum,
    new_weights,
    new_first,
    new_second,
    base_new,
    outer_new,
    order_ref,
    cot_raw,
    cot,
    tok,
    tok_stage,
    sent,
    got,
    weights_v,
    first_v,
    second_v,
    base_v,
    outer_v,
    weights_p,
    first_p,
    second_p,
    frag,
    frag_got,
    base_sent,
    base_all,
    plan_load,
    cot_load,
    own_load,
    stage_load,
    state_load,
    y_send_cot,
    y_recv_cot,
    y_send_tok,
    y_recv_tok,
    z_send,
    z_recv,
    frag_send,
    frag_recv,
    base_send,
    base_recv,
):
    island = lax.axis_index("island")
    fsdp = lax.axis_index("fsdp")
    islands = lax.axis_size("island")
    z = fsdp // 2
    h = fsdp % 2
    partner = (island, z * 2 + (1 - h))
    up = (island, ((z + 1) % Z) * 2 + h)
    down = (island, ((z + Z - 1) % Z) * 2 + h)
    deltas = (4, 3, 5, 2, 6, 1, 7, 0)
    token_order = tuple((s, r) for pair in ((0,), (1, 2), (3, 4), (5, 6), (7,)) for r in range(2) for s in pair)

    cot_copy = pltpu.make_async_copy(cotangent, cot_raw, cot_load)

    def own_copy(s, r):
        column = ((z + deltas[s]) % Z * 2 + h) * 2 * HALF + r * HALF
        return pltpu.make_async_copy(
            tokens.at[:, pl.ds(pl.multiple_of(column, HALF), HALF)],
            tok.at[s, r, pl.ds(0, HALF), :],
            own_load.at[s, r],
        )

    def stage_copy(s, r):
        column = ((z + deltas[s]) % Z * 2 + (1 - h)) * 2 * HALF + r * HALF
        return pltpu.make_async_copy(
            tokens.at[:, pl.ds(pl.multiple_of(column, HALF), HALF)],
            tok_stage.at[s, r],
            stage_load.at[s, r],
        )

    def y_cot(g):
        return pltpu.make_async_remote_copy(
            cot.at[g, pl.ds(0, HALF), :],
            cot.at[g, pl.ds(HALF, HALF), :],
            y_send_cot.at[g],
            y_recv_cot.at[g],
            device_id=partner,
            device_id_type=MESH,
        )

    def y_tok(s, r, q=0, size=HALF):
        part = pl.ds(q * EIGHTH, size)
        return pltpu.make_async_remote_copy(
            tok_stage.at[s, r, :, part],
            tok.at[s, r, pl.ds(HALF, HALF), part],
            y_send_tok.at[s, r, q],
            y_recv_tok.at[s, r, q],
            device_id=partner,
            device_id_type=MESH,
        )

    plan = pltpu.make_async_copy(order, order_ref, plan_load)
    plan.start()
    cot_copy.start()
    for s, r in token_order[:2]:
        stage_copy(s, r).start()
    barrier = pltpu.get_barrier_semaphore()
    for peer in (partner, up, down):
        pl.semaphore_signal(barrier, inc=1, device_id=peer, device_id_type=MESH)

    def greet(k, carry):
        pl.semaphore_signal(
            barrier, inc=1, device_id=(lax.rem(island + k, islands), fsdp), device_id_type=MESH
        )
        return carry

    lax.fori_loop(1, islands, greet, 0)
    for s, r in token_order[2:6]:
        stage_copy(s, r).start()
    for s, r in token_order[:2]:
        own_copy(s, r).start()

    plan.wait()
    first_part = step_ref[0] == 0

    def head_of(j):
        return jnp.where(first_part, order_ref[j], order_ref[lax.rem(j + SYNC, KVH)])

    def columns_of(head, source, rows):
        found = source[rows, 0:HD]
        for other in range(1, KVH):
            found = lax.select(head == other, source[rows, other * HD : (other + 1) * HD], found)
        return found

    def sort_cot(g):
        for j in (2 * g, 2 * g + 1):
            cot[g, 0:HALF, (j % 2) * HD : (j % 2 + 1) * HD] = columns_of(
                head_of(j), cot_raw, slice(0, HALF)
            )

    def send_tok(s, r):
        stage_copy(s, r).wait()
        y_tok(s, r).start()

    cot_copy.wait()
    sort_cot(0)
    pl.semaphore_wait(barrier, 3 + islands - 1)
    send_tok(0, 0)
    y_cot(0).start()
    send_tok(0, 1)
    sort_cot(1)
    y_cot(1).start()
    for s, r in token_order[2:6]:
        own_copy(s, r).start()
    for s, r in token_order[6:]:
        stage_copy(s, r).start()
    sort_cot(2)
    sort_cot(3)
    for r in range(2):
        for s in (1, 2):
            stage_copy(s, r).wait()
        for q in range(2):
            for s in (1, 2):
                y_tok(s, r, q, EIGHTH).start()
            if r != q:
                y_cot(2 + r).start()
    for s, r in token_order[6:]:
        own_copy(s, r).start()
    for s, r in token_order[6:]:
        send_tok(s, r)
    state = [
        pltpu.make_async_copy(src, dst, state_load.at[i])
        for i, (src, dst) in enumerate(
            (
                (params, weights_v),
                (first_moment, first_v),
                (second_moment, second_v),
                (base, base_v),
                (outer_momentum, outer_v),
            )
        )
    ]
    for copy in state:
        copy.start()

    def z_copy(way, stage, g, r, low=0, size=HALF):
        rows = pl.ds(low, size)
        return pltpu.make_async_remote_copy(
            sent.at[way, stage, g, r, rows, :],
            got.at[way, stage, g, r, rows, :],
            z_send.at[way, stage, g, r],
            z_recv.at[way, stage, g, r],
            device_id=(up, down)[way],
            device_id_type=MESH,
        )

    def need_tok(s, r):
        own_copy(s, r).wait()
        y_tok(s, r).wait_recv()

    def need_cot(g):
        y_cot(g).wait_recv()

    def term(s, g, r):
        return partial_product(tok[s, r], cot[g])

    def pass_on(way, stage, s, g, r):
        total = term(s, g, r)
        z_copy(way, stage - 1, g, r).wait_recv()
        total = total + got[way, stage - 1, g, r].astype(F32)
        sent[way, stage, g, r] = total.astype(BF16)
        z_copy(way, stage, g, r).start()

    def ends(g, r):
        sent[0, 0, g, r] = term(0, g, r).astype(BF16)
        for way in range(2):
            rows = pl.ds(way * EIGHTH, EIGHTH)
            pltpu.make_async_remote_copy(
                sent.at[0, 0, g, r, rows, :],
                got.at[way, 0, g, r, rows, :],
                z_send.at[way, 0, g, r],
                z_recv.at[way, 0, g, r],
                device_id=(up, down)[way],
                device_id_type=MESH,
            ).start()

    def third_half(way, q, g, r):
        rows = slice(q * EIGHTH, (q + 1) * EIGHTH)
        total = partial_product(tok[1 + way, r, :, rows], cot[g])
        if q == way:
            z_copy(way, 0, g, r, q * EIGHTH, EIGHTH).wait_recv()
            total = total + got[way, 0, g, r, rows, :].astype(F32)
        sent[way, 1, g, r, rows, :] = total.astype(BF16)
        z_copy(way, 1, g, r, q * EIGHTH, EIGHTH).start()

    def third(q, r, low, count):
        def body(g, carry):
            for way in range(2):
                third_half(way, q, g, r)
            return carry

        lax.fori_loop(low, low + count, body, 0)

    def middle_first(stage):
        s_up, s_down = 2 * stage - 1, 2 * stage
        for r in range(2):
            need_tok(s_up, r)
            need_tok(s_down, r)

            def body(g, carry, r=r):
                pass_on(0, stage, s_up, g, r)
                pass_on(1, stage, s_down, g, r)
                return carry

            lax.fori_loop(0, 2, body, 0)

    def middle(stage, g):
        def body(r, carry):
            pass_on(0, stage, 2 * stage - 1, g, r)
            pass_on(1, stage, 2 * stage, g, r)
            return carry

        lax.fori_loop(0, 2, body, 0)

    def sort_heads(low):
        def body(item, carry):
            j = low + item // 2
            rows = pl.ds(pl.multiple_of(item % 2 * HALF, HALF), HALF)
            head = head_of(j)
            weights_p[j, rows, :] = columns_of(head, weights_v, rows)
            first_p[j, rows, :] = columns_of(head, first_v, rows)
            second_p[j, rows, :] = columns_of(head, second_v, rows)
            return carry

        lax.fori_loop(0, 2 * SYNC, body, 0)

    def own_rows(low, fragment, first_item, last_item):
        def body(item, carry):
            r = item % 2
            g = low + item // 2
            rows = pl.ds(pl.multiple_of(r * HALF, HALF), HALF)
            grad = term(7, g, r)
            for way in range(2):
                z_copy(way, 3, g, r).wait_recv()
                grad = grad + got[way, 3, g, r].astype(F32)
            for k in range(2):
                j = 2 * g + k
                part = grad[:, k * HD : (k + 1) * HD]
                one = 0.9 * first_p[j, rows, :].astype(F32) + 0.1 * part
                two = 0.95 * second_p[j, rows, :].astype(F32) + 0.05 * part * part
                weights = weights_p[j, rows, :]
                stepped = weights - 0.01 * (one / (jnp.sqrt(two) + 1e-08) + 0.1 * weights)
                new_first[j, rows, :] = one.astype(BF16)
                new_second[j, rows, :] = two.astype(BF16)
                if fragment:
                    frag[rows, pl.ds(pl.multiple_of(j * HD, HD), HD)] = stepped.astype(BF16)
                else:
                    new_weights[j, rows, :] = stepped
            return carry

        lax.fori_loop(first_item, last_item, body, 0)

    share = base.shape[0]

    def frag_copy(k):
        peer = lax.rem(island + k, islands)
        return pltpu.make_async_remote_copy(
            frag.at[pl.ds(pl.multiple_of(peer * share, share), share), :],
            frag_got.at[k],
            frag_send.at[k],
            frag_recv.at[k],
            device_id=(peer, fsdp),
            device_id_type=MESH,
        )

    def base_copy(k):
        return pltpu.make_async_remote_copy(
            base_sent,
            base_all.at[pl.ds(pl.multiple_of(island * share, share), share), :],
            base_send.at[k],
            base_recv.at[k],
            device_id=(lax.rem(island + k, islands), fsdp),
            device_id_type=MESH,
        )

    def each_peer(action):
        def body(k, carry):
            action(k)
            return carry

        lax.fori_loop(1, islands, body, 0)

    def outer_step():
        mine = pl.ds(pl.multiple_of(island * share, share), share)

        def add(k, total):
            frag_copy(k).wait_recv()
            return total + frag_got[k].astype(F32)

        total = lax.fori_loop(1, islands, add, frag[mine, :].astype(F32))
        delta = base_v[...] - total / islands
        momentum = 0.9 * outer_v[...] + delta
        following = base_v[...] - 0.7 * (delta + 0.9 * momentum)
        base_sent[...] = following.astype(BF16)
        base_all[mine, :] = following.astype(BF16)
        base_new[...] = following
        outer_new[...] = momentum
        each_peer(lambda k: base_copy(k).start())

    need_cot(0)
    for r in range(2):
        need_tok(0, r)
        ends(0, r)
    need_cot(1)
    for r in range(2):
        ends(1, r)

    def need_third(q, r):
        for s in (1, 2):
            if q == 0:
                own_copy(s, r).wait()
            y_tok(s, r, q, EIGHTH).wait_recv()

    for q in range(2):
        need_third(q, 0)
        third(q, 0, 0, 2)
    need_cot(2)
    for r in range(2):
        ends(2, r)
    for q in range(2):
        third(q, 0, 2, 1)
    for q in range(2):
        need_third(q, 1)
        third(q, 1, 0, 3)
    need_cot(3)
    for r in range(2):
        ends(3, r)
    for copy in state:
        copy.wait()
    sort_heads(0)
    middle_first(2)
    middle_first(3)
    for r in range(2):
        for q in range(2):
            third(q, r, 3, 1)
    middle(2, 2)
    sort_heads(SYNC)
    need_tok(7, 0)
    need_tok(7, 1)
    own_rows(0, True, 0, 4)
    each_peer(lambda k: frag_copy(k).start())
    middle(2, 3)
    middle(3, 2)
    outer_step()
    middle(3, 3)
    own_rows(2, False, 0, 2)
    each_peer(lambda k: base_copy(k).wait_recv())
    for j in range(SYNC):
        new_weights[j] = base_all[:, j * HD : (j + 1) * HD].astype(F32)
    own_rows(2, False, 2, 4)

    for g in range(4):
        y_cot(g).wait_send()
    for s, r in token_order:
        if s in (1, 2):
            for q in range(2):
                y_tok(s, r, q, EIGHTH).wait_send()
        else:
            y_tok(s, r).wait_send()

    def leaf_sends(item, carry):
        for way in range(2):
            z_copy(way, 0, item // 2, item % 2, way * EIGHTH, EIGHTH).wait_send()
        return carry

    lax.fori_loop(0, 8, leaf_sends, 0)

    def sends(item, carry):
        for way in range(2):
            z_copy(way, 1 + item // 8, item // 2 % 4, item % 2).wait_send()
        return carry

    lax.fori_loop(0, 24, sends, 0)
    each_peer(lambda k: frag_copy(k).wait_send())
    each_peer(lambda k: base_copy(k).wait_send())


def placing_kernel(
    order,
    step_ref,
    weights,
    first,
    second,
    base,
    momentum,
    w_out,
    f_out,
    s_out,
    b_out,
    m_out,
    order_ref,
    plan_load,
    sems,
):
    plan = pltpu.make_async_copy(order, order_ref, plan_load)
    plan.start()
    copies = []
    for i, (source, out) in enumerate(((base, b_out), (momentum, m_out))):
        copies.append(pltpu.make_async_copy(source, out, sems.at[3, i]))
        copies[-1].start()
    plan.wait()
    for head in range(KVH):
        place = 0
        for j in range(1, KVH):
            found = order_ref[lax.rem(step_ref[0] * SYNC + j, KVH)] == head
            place = place + jnp.where(found, j, 0)
        columns = pl.ds(head * HD, HD)
        for i, (source, out) in enumerate(((weights, w_out), (first, f_out), (second, s_out))):
            copies.append(
                pltpu.make_async_copy(source.at[place], out.at[:, columns], sems.at[i, head])
            )
            copies[-1].start()
    for copy in copies:
        copy.wait()


def shards(
    tokens,
    cotangent,
    params,
    first_moment,
    second_moment,
    base,
    outer_momentum,
    head_order,
    step_fragment,
):
    rows, width = params.shape[1:]
    share, columns = base.shape
    islands = lax.axis_size("island")
    smem = pl.BlockSpec(memory_space=pltpu.SMEM)
    anywhere = pl.BlockSpec(memory_space=pl.ANY)
    dma = pltpu.SemaphoreType.DMA

    def in_hbm(x):
        return pltpu.with_memory_space_constraint(x, pltpu.HBM)

    made = pl.pallas_call(
        sync_kernel,
        name="inner_step_and_outer_sync",
        out_shape=(
            pltpu.VMEM((KVH, rows, HD), F32),
            pltpu.VMEM((KVH, rows, HD), BF16),
            pltpu.VMEM((KVH, rows, HD), BF16),
            pltpu.VMEM((share, columns), F32),
            pltpu.VMEM((share, columns), F32),
        ),
        in_specs=[anywhere, smem] + [anywhere] * 7,
        out_specs=(pl.BlockSpec(memory_space=pltpu.VMEM),) * 5,
        scratch_shapes=[
            pltpu.SMEM((KVH,), jnp.int32),
            pltpu.VMEM((HALF, width), BF16),
            pltpu.VMEM((4, 2 * HALF, GC), BF16),
            pltpu.VMEM((Z, 2, 2 * HALF, HALF), BF16),
            pltpu.VMEM((Z, 2, HALF, HALF), BF16),
            pltpu.VMEM((2, 4, 4, 2, HALF, GC), BF16),
            pltpu.VMEM((2, 4, 4, 2, HALF, GC), BF16),
            pltpu.VMEM((rows, width), F32),
            pltpu.VMEM((rows, width), BF16),
            pltpu.VMEM((rows, width), BF16),
            pltpu.VMEM((share, columns), F32),
            pltpu.VMEM((share, columns), F32),
            pltpu.VMEM((KVH, rows, HD), F32),
            pltpu.VMEM((KVH, rows, HD), BF16),
            pltpu.VMEM((KVH, rows, HD), BF16),
            pltpu.VMEM((rows, columns), BF16),
            pltpu.VMEM((16, share, columns), BF16),
            pltpu.VMEM((share, columns), BF16),
            pltpu.VMEM((rows, columns), BF16),
            dma,
            dma,
            dma((Z, 2)),
            dma((Z, 2)),
            dma((5,)),
            dma((4,)),
            dma((4,)),
            dma((Z, 2, 2)),
            dma((Z, 2, 2)),
            dma((2, 4, 4, 2)),
            dma((2, 4, 4, 2)),
            dma((16,)),
            dma((16,)),
            dma((16,)),
            dma((16,)),
        ],
        compiler_params=pltpu.CompilerParams(
            collective_id=0, has_side_effects=True, vmem_limit_bytes=48 * 2**20
        ),
        cost_estimate=pl.CostEstimate(
            flops=2 * 256 * 8192 * 1024, bytes_accessed=13 * 2**20, transcendentals=rows * width
        ),
    )(
        in_hbm(head_order),
        step_fragment,
        in_hbm(tokens[0]),
        in_hbm(cotangent[0]),
        in_hbm(params[0]),
        in_hbm(first_moment[0]),
        in_hbm(second_moment[0]),
        in_hbm(base),
        in_hbm(outer_momentum),
    )
    weights, first, second, base_next, momentum_next = pl.pallas_call(
        placing_kernel,
        name="heads_in_place",
        out_shape=(
            jax.ShapeDtypeStruct((rows, width), F32),
            jax.ShapeDtypeStruct((rows, width), BF16),
            jax.ShapeDtypeStruct((rows, width), BF16),
            jax.ShapeDtypeStruct((share, columns), F32),
            jax.ShapeDtypeStruct((share, columns), F32),
        ),
        in_specs=[anywhere, smem] + [anywhere] * 5,
        out_specs=(anywhere,) * 5,
        scratch_shapes=[
            pltpu.SMEM((KVH,), jnp.int32),
            dma,
            dma((4, KVH)),
        ],
        compiler_params=pltpu.CompilerParams(vmem_limit_bytes=4 * 2**20),
    )(
        in_hbm(head_order),
        step_fragment,
        *(pltpu.with_memory_space_constraint(x, pltpu.VMEM) for x in made),
    )
    return (weights[None], first[None], second[None], base_next, momentum_next)


def solution(mesh):
    placed = (
        P("island", "fsdp", None),
        P("island", "fsdp", None),
        P("island", "fsdp", None),
        P("island", "fsdp", None),
        P("island", "fsdp", None),
        P(("fsdp", "island"), None),
        P(("fsdp", "island"), None),
        P(),
        P(),
    )
    return jax.shard_map(
        shards,
        mesh=mesh,
        in_specs=placed,
        out_specs=(
            P("island", "fsdp", None),
            P("island", "fsdp", None),
            P("island", "fsdp", None),
            P(("fsdp", "island"), None),
            P(("fsdp", "island"), None),
        ),
        check_vma=False,
    )
```

```python
import functools

import jax
import jax.numpy as jnp
from jax import lax
from jax.experimental import pallas as pl
from jax.experimental.pallas import tpu as pltpu
from jax.sharding import PartitionSpec as P

KVH = 8
HD = 128
SYNC = 4
Z = 8
HALF = 256
EIGHTH = 128
GC = 256
MESH = pl.DeviceIdType.MESH
F32 = jnp.float32
BF16 = jnp.bfloat16


def partial_product(a, b):
    return lax.dot_general(a, b, (((0,), (0,)), ((), ())), preferred_element_type=F32)


def sync_kernel(
    order,
    step_ref,
    tokens,
    cotangent,
    params,
    first_moment,
    second_moment,
    base,
    outer_momentum,
    new_weights,
    new_first,
    new_second,
    base_new,
    outer_new,
    order_ref,
    cot_raw,
    cot,
    tok,
    tok_stage,
    sent,
    got,
    side_sent,
    side_got,
    side_all,
    weights_v,
    first_v,
    second_v,
    base_v,
    outer_v,
    weights_p,
    first_p,
    second_p,
    frag,
    frag_got,
    base_sent,
    base_all,
    plan_load,
    cot_load,
    own_load,
    stage_load,
    state_load,
    y_send_cot,
    y_recv_cot,
    y_send_tok,
    y_recv_tok,
    z_send,
    z_recv,
    side_send,
    side_recv,
    cross_send,
    cross_recv,
    frag_send,
    frag_recv,
    base_send,
    base_recv,
):
    island = lax.axis_index("island")
    fsdp = lax.axis_index("fsdp")
    islands = lax.axis_size("island")
    z = fsdp // 2
    h = fsdp % 2
    partner = (island, z * 2 + (1 - h))
    up = (island, ((z + 1) % Z) * 2 + h)
    down = (island, ((z + Z - 1) % Z) * 2 + h)
    deltas = (4, 3, 5, 2, 6, 1, 7, 0)
    token_order = tuple((s, r) for pair in ((0,), (1, 2), (3, 4), (5, 6), (7,)) for r in range(2) for s in pair)

    cot_copy = pltpu.make_async_copy(cotangent, cot_raw, cot_load)

    def own_copy(s, r):
        column = ((z + deltas[s]) % Z * 2 + h) * 2 * HALF + r * HALF
        return pltpu.make_async_copy(
            tokens.at[:, pl.ds(pl.multiple_of(column, HALF), HALF)],
            tok.at[s, r, pl.ds(0, HALF), :],
            own_load.at[s, r],
        )

    def stage_copy(s, r):
        column = ((z + deltas[s]) % Z * 2 + (1 - h)) * 2 * HALF + r * HALF
        return pltpu.make_async_copy(
            tokens.at[:, pl.ds(pl.multiple_of(column, HALF), HALF)],
            tok_stage.at[s, r],
            stage_load.at[s, r],
        )

    def y_cot(g):
        return pltpu.make_async_remote_copy(
            cot.at[g, pl.ds(0, HALF), :],
            cot.at[g, pl.ds(HALF, HALF), :],
            y_send_cot.at[g],
            y_recv_cot.at[g],
            device_id=partner,
            device_id_type=MESH,
        )

    def y_tok(s, r, q=0, size=HALF):
        part = pl.ds(q * EIGHTH, size)
        return pltpu.make_async_remote_copy(
            tok_stage.at[s, r, :, part],
            tok.at[s, r, pl.ds(HALF, HALF), part],
            y_send_tok.at[s, r, q],
            y_recv_tok.at[s, r, q],
            device_id=partner,
            device_id_type=MESH,
        )

    plan = pltpu.make_async_copy(order, order_ref, plan_load)
    plan.start()
    cot_copy.start()
    for s, r in token_order[:2]:
        stage_copy(s, r).start()
    barrier = pltpu.get_barrier_semaphore()
    for peer in (partner, up, down):
        pl.semaphore_signal(barrier, inc=1, device_id=peer, device_id_type=MESH)

    def greet(k, carry):
        pl.semaphore_signal(
            barrier, inc=1, device_id=(lax.rem(island + k, islands), fsdp), device_id_type=MESH
        )
        return carry

    lax.fori_loop(1, islands, greet, 0)
    for s, r in token_order[2:6]:
        stage_copy(s, r).start()
    for s, r in token_order[:2]:
        own_copy(s, r).start()

    plan.wait()
    first_part = step_ref[0] == 0

    def head_of(j):
        return jnp.where(first_part, order_ref[j], order_ref[lax.rem(j + SYNC, KVH)])

    def columns_of(head, source, rows):
        found = source[rows, 0:HD]
        for other in range(1, KVH):
            found = lax.select(head == other, source[rows, other * HD : (other + 1) * HD], found)
        return found

    def side_copy(way, r):
        return pltpu.make_async_remote_copy(
            side_sent.at[r, pl.ds(way * EIGHTH, EIGHTH), :],
            side_got.at[way, r],
            side_send.at[way, r],
            side_recv.at[way, r],
            device_id=(up, down)[way],
            device_id_type=MESH,
        )

    def cross_copy(way, r):
        return pltpu.make_async_remote_copy(
            side_got.at[way, r],
            side_all.at[way, r],
            cross_send.at[way, r],
            cross_recv.at[way, r],
            device_id=partner,
            device_id_type=MESH,
        )

    def leaf_copy(way, g, r):
        rows = pl.ds(way * EIGHTH, EIGHTH)
        return pltpu.make_async_remote_copy(
            sent.at[0, 0, g, r, rows, :],
            got.at[way, 0, g, r, rows, :],
            z_send.at[way, 0, g, r],
            z_recv.at[way, 0, g, r],
            device_id=(up, down)[way],
            device_id_type=MESH,
        )

    def early_ends(g):
        for r in range(2):
            own_copy(0, r).wait()
            mine = cot[g, 0:HALF, :]
            sent[0, 0, g, r] = partial_product(tok[0, r, 0:HALF, :], mine).astype(BF16)
            for way in range(2):
                leaf_copy(way, g, r).start()
            side_sent[r] = partial_product(tok_stage[0, r], mine).astype(BF16)
            for way in range(2):
                side_copy(way, r).start()

    def sort_cot(g):
        for j in (2 * g, 2 * g + 1):
            cot[g, 0:HALF, (j % 2) * HD : (j % 2 + 1) * HD] = columns_of(
                head_of(j), cot_raw, slice(0, HALF)
            )

    def send_tok(s, r):
        stage_copy(s, r).wait()
        y_tok(s, r).start()

    cot_copy.wait()
    sort_cot(0)
    pl.semaphore_wait(barrier, 3 + islands - 1)
    send_tok(0, 0)
    y_cot(0).start()
    send_tok(0, 1)
    sort_cot(1)
    y_cot(1).start()
    sort_cot(3)
    early_ends(3)
    for s, r in token_order[2:6]:
        own_copy(s, r).start()
    for s, r in token_order[6:]:
        stage_copy(s, r).start()
    sort_cot(2)
    for r in range(2):
        for s in (1, 2):
            stage_copy(s, r).wait()
        for q in range(2):
            for s in (1, 2):
                y_tok(s, r, q, EIGHTH).start()
            if r != q:
                y_cot(2 + r).start()
    for s, r in token_order[6:]:
        own_copy(s, r).start()
    for s, r in token_order[6:14]:
        send_tok(s, r)
    state = [
        pltpu.make_async_copy(src, dst, state_load.at[i])
        for i, (src, dst) in enumerate(
            (
                (params, weights_v),
                (first_moment, first_v),
                (second_moment, second_v),
                (base, base_v),
                (outer_momentum, outer_v),
            )
        )
    ]
    for copy in state:
        copy.start()

    def z_copy(way, stage, g, r, low=0, size=HALF):
        rows = pl.ds(low, size)
        return pltpu.make_async_remote_copy(
            sent.at[way, stage, g, r, rows, :],
            got.at[way, stage, g, r, rows, :],
            z_send.at[way, stage, g, r],
            z_recv.at[way, stage, g, r],
            device_id=(up, down)[way],
            device_id_type=MESH,
        )

    def need_tok(s, r):
        own_copy(s, r).wait()
        y_tok(s, r).wait_recv()

    def need_cot(g):
        y_cot(g).wait_recv()

    def term(s, g, r):
        return partial_product(tok[s, r], cot[g])

    def pass_on(way, stage, s, g, r):
        total = term(s, g, r)
        z_copy(way, stage - 1, g, r).wait_recv()
        total = total + got[way, stage - 1, g, r].astype(F32)
        sent[way, stage, g, r] = total.astype(BF16)
        z_copy(way, stage, g, r).start()

    def ends(g, r):
        sent[0, 0, g, r] = term(0, g, r).astype(BF16)
        for way in range(2):
            leaf_copy(way, g, r).start()

    def third_half(way, q, g, r, early):
        rows = slice(q * EIGHTH, (q + 1) * EIGHTH)
        total = partial_product(tok[1 + way, r, :, rows], cot[g])
        if q == way:
            z_copy(way, 0, g, r, q * EIGHTH, EIGHTH).wait_recv()
            total = total + got[way, 0, g, r, rows, :].astype(F32)
            if early:
                cross_copy(way, r).wait_recv()
                total = total + side_all[way, r].astype(F32)
        sent[way, 1, g, r, rows, :] = total.astype(BF16)
        z_copy(way, 1, g, r, q * EIGHTH, EIGHTH).start()

    def third(q, r, low, count, early=False):
        def body(g, carry):
            for way in range(2):
                third_half(way, q, g, r, early)
            return carry

        lax.fori_loop(low, low + count, body, 0)

    def middle_first(stage):
        s_up, s_down = 2 * stage - 1, 2 * stage
        for r in range(2):
            need_tok(s_up, r)
            need_tok(s_down, r)

            def body(g, carry, r=r):
                pass_on(0, stage, s_up, g, r)
                pass_on(1, stage, s_down, g, r)
                return carry

            lax.fori_loop(0, 2, body, 0)

    def middle(stage, g):
        def body(r, carry):
            pass_on(0, stage, 2 * stage - 1, g, r)
            pass_on(1, stage, 2 * stage, g, r)
            return carry

        lax.fori_loop(0, 2, body, 0)

    def sort_heads(low):
        def body(item, carry):
            j = low + item // 2
            rows = pl.ds(pl.multiple_of(item % 2 * HALF, HALF), HALF)
            head = head_of(j)
            weights_p[j, rows, :] = columns_of(head, weights_v, rows)
            first_p[j, rows, :] = columns_of(head, first_v, rows)
            second_p[j, rows, :] = columns_of(head, second_v, rows)
            return carry

        lax.fori_loop(0, 2 * SYNC, body, 0)

    def own_rows(low, fragment, first_item, last_item):
        def body(item, carry):
            r = item % 2
            g = low + item // 2
            rows = pl.ds(pl.multiple_of(r * HALF, HALF), HALF)
            grad = term(7, g, r)
            for way in range(2):
                z_copy(way, 3, g, r).wait_recv()
                grad = grad + got[way, 3, g, r].astype(F32)
            for k in range(2):
                j = 2 * g + k
                part = grad[:, k * HD : (k + 1) * HD]
                one = 0.9 * first_p[j, rows, :].astype(F32) + 0.1 * part
                two = 0.95 * second_p[j, rows, :].astype(F32) + 0.05 * part * part
                weights = weights_p[j, rows, :]
                stepped = weights - 0.01 * (one / (jnp.sqrt(two) + 1e-08) + 0.1 * weights)
                new_first[j, rows, :] = one.astype(BF16)
                new_second[j, rows, :] = two.astype(BF16)
                if fragment:
                    frag[rows, pl.ds(pl.multiple_of(j * HD, HD), HD)] = stepped.astype(BF16)
                else:
                    new_weights[j, rows, :] = stepped
            return carry

        lax.fori_loop(first_item, last_item, body, 0)

    share = base.shape[0]

    def frag_copy(k):
        peer = lax.rem(island + k, islands)
        return pltpu.make_async_remote_copy(
            frag.at[pl.ds(pl.multiple_of(peer * share, share), share), :],
            frag_got.at[k],
            frag_send.at[k],
            frag_recv.at[k],
            device_id=(peer, fsdp),
            device_id_type=MESH,
        )

    def base_copy(k):
        return pltpu.make_async_remote_copy(
            base_sent,
            base_all.at[pl.ds(pl.multiple_of(island * share, share), share), :],
            base_send.at[k],
            base_recv.at[k],
            device_id=(lax.rem(island + k, islands), fsdp),
            device_id_type=MESH,
        )

    def each_peer(action):
        def body(k, carry):
            action(k)
            return carry

        lax.fori_loop(1, islands, body, 0)

    def outer_step():
        mine = pl.ds(pl.multiple_of(island * share, share), share)

        def add(k, total):
            frag_copy(k).wait_recv()
            return total + frag_got[k].astype(F32)

        total = lax.fori_loop(1, islands, add, frag[mine, :].astype(F32))
        delta = base_v[...] - total / islands
        momentum = 0.9 * outer_v[...] + delta
        following = base_v[...] - 0.7 * (delta + 0.9 * momentum)
        base_sent[...] = following.astype(BF16)
        base_all[mine, :] = following.astype(BF16)
        base_new[...] = following
        outer_new[...] = momentum
        each_peer(lambda k: base_copy(k).start())

    need_cot(0)
    for r in range(2):
        y_tok(0, r).wait_recv()
        ends(0, r)
    need_cot(1)
    for r in range(2):
        ends(1, r)

    def need_third(q, r):
        for s in (1, 2):
            if q == 0:
                own_copy(s, r).wait()
            y_tok(s, r, q, EIGHTH).wait_recv()

    for q in range(2):
        need_third(q, 0)
        third(q, 0, 0, 2)
    for r in range(2):
        for way in range(2):
            side_copy(way, r).wait_recv()
            cross_copy(way, r).start()
    for r in range(2):
        send_tok(7, r)
    need_cot(2)
    for r in range(2):
        ends(2, r)
    for q in range(2):
        third(q, 0, 2, 1)
    for q in range(2):
        need_third(q, 1)
        third(q, 1, 0, 3)
    need_cot(3)
    for copy in state:
        copy.wait()
    sort_heads(0)
    middle_first(2)
    middle_first(3)
    for r in range(2):
        for q in range(2):
            third(q, r, 3, 1, True)
    middle(2, 2)
    sort_heads(SYNC)
    need_tok(7, 0)
    need_tok(7, 1)
    own_rows(0, True, 0, 4)
    each_peer(lambda k: frag_copy(k).start())
    middle(2, 3)
    middle(3, 2)
    outer_step()
    middle(3, 3)
    own_rows(2, False, 0, 2)
    each_peer(lambda k: base_copy(k).wait_recv())
    for j in range(SYNC):
        new_weights[j] = base_all[:, j * HD : (j + 1) * HD].astype(F32)
    own_rows(2, False, 2, 4)

    for g in range(4):
        y_cot(g).wait_send()
    for s, r in token_order:
        if s in (1, 2):
            for q in range(2):
                y_tok(s, r, q, EIGHTH).wait_send()
        else:
            y_tok(s, r).wait_send()

    for r in range(2):
        for way in range(2):
            side_copy(way, r).wait_send()
            cross_copy(way, r).wait_send()

    def leaf_sends(item, carry):
        for way in range(2):
            z_copy(way, 0, item // 2, item % 2, way * EIGHTH, EIGHTH).wait_send()
        return carry

    lax.fori_loop(0, 8, leaf_sends, 0)

    def sends(item, carry):
        for way in range(2):
            z_copy(way, 1 + item // 8, item // 2 % 4, item % 2).wait_send()
        return carry

    lax.fori_loop(0, 24, sends, 0)
    each_peer(lambda k: frag_copy(k).wait_send())
    each_peer(lambda k: base_copy(k).wait_send())


def placing_kernel(
    order,
    step_ref,
    weights,
    first,
    second,
    base,
    momentum,
    w_out,
    f_out,
    s_out,
    b_out,
    m_out,
    order_ref,
    plan_load,
    sems,
):
    plan = pltpu.make_async_copy(order, order_ref, plan_load)
    plan.start()
    copies = []
    for i, (source, out) in enumerate(((base, b_out), (momentum, m_out))):
        copies.append(pltpu.make_async_copy(source, out, sems.at[3, i]))
        copies[-1].start()
    plan.wait()
    for head in range(KVH):
        place = 0
        for j in range(1, KVH):
            found = order_ref[lax.rem(step_ref[0] * SYNC + j, KVH)] == head
            place = place + jnp.where(found, j, 0)
        columns = pl.ds(head * HD, HD)
        for i, (source, out) in enumerate(((weights, w_out), (first, f_out), (second, s_out))):
            copies.append(
                pltpu.make_async_copy(source.at[place], out.at[:, columns], sems.at[i, head])
            )
            copies[-1].start()
    for copy in copies:
        copy.wait()


def shards(
    tokens,
    cotangent,
    params,
    first_moment,
    second_moment,
    base,
    outer_momentum,
    head_order,
    step_fragment,
):
    rows, width = params.shape[1:]
    share, columns = base.shape
    islands = lax.axis_size("island")
    smem = pl.BlockSpec(memory_space=pltpu.SMEM)
    anywhere = pl.BlockSpec(memory_space=pl.ANY)
    dma = pltpu.SemaphoreType.DMA

    def in_hbm(x):
        return pltpu.with_memory_space_constraint(x, pltpu.HBM)

    made = pl.pallas_call(
        sync_kernel,
        name="inner_step_and_outer_sync",
        out_shape=(
            pltpu.VMEM((KVH, rows, HD), F32),
            pltpu.VMEM((KVH, rows, HD), BF16),
            pltpu.VMEM((KVH, rows, HD), BF16),
            pltpu.VMEM((share, columns), F32),
            pltpu.VMEM((share, columns), F32),
        ),
        in_specs=[anywhere, smem] + [anywhere] * 7,
        out_specs=(pl.BlockSpec(memory_space=pltpu.VMEM),) * 5,
        scratch_shapes=[
            pltpu.SMEM((KVH,), jnp.int32),
            pltpu.VMEM((HALF, width), BF16),
            pltpu.VMEM((4, 2 * HALF, GC), BF16),
            pltpu.VMEM((Z, 2, 2 * HALF, HALF), BF16),
            pltpu.VMEM((Z, 2, HALF, HALF), BF16),
            pltpu.VMEM((2, 4, 4, 2, HALF, GC), BF16),
            pltpu.VMEM((2, 4, 4, 2, HALF, GC), BF16),
            pltpu.VMEM((2, HALF, GC), BF16),
            pltpu.VMEM((2, 2, EIGHTH, GC), BF16),
            pltpu.VMEM((2, 2, EIGHTH, GC), BF16),
            pltpu.VMEM((rows, width), F32),
            pltpu.VMEM((rows, width), BF16),
            pltpu.VMEM((rows, width), BF16),
            pltpu.VMEM((share, columns), F32),
            pltpu.VMEM((share, columns), F32),
            pltpu.VMEM((KVH, rows, HD), F32),
            pltpu.VMEM((KVH, rows, HD), BF16),
            pltpu.VMEM((KVH, rows, HD), BF16),
            pltpu.VMEM((rows, columns), BF16),
            pltpu.VMEM((16, share, columns), BF16),
            pltpu.VMEM((share, columns), BF16),
            pltpu.VMEM((rows, columns), BF16),
            dma,
            dma,
            dma((Z, 2)),
            dma((Z, 2)),
            dma((5,)),
            dma((4,)),
            dma((4,)),
            dma((Z, 2, 2)),
            dma((Z, 2, 2)),
            dma((2, 4, 4, 2)),
            dma((2, 4, 4, 2)),
            dma((2, 2)),
            dma((2, 2)),
            dma((2, 2)),
            dma((2, 2)),
            dma((16,)),
            dma((16,)),
            dma((16,)),
            dma((16,)),
        ],
        compiler_params=pltpu.CompilerParams(
            collective_id=0, has_side_effects=True, vmem_limit_bytes=48 * 2**20
        ),
        cost_estimate=pl.CostEstimate(
            flops=2 * 256 * 8192 * 1024, bytes_accessed=13 * 2**20, transcendentals=rows * width
        ),
    )(
        in_hbm(head_order),
        step_fragment,
        in_hbm(tokens[0]),
        in_hbm(cotangent[0]),
        in_hbm(params[0]),
        in_hbm(first_moment[0]),
        in_hbm(second_moment[0]),
        in_hbm(base),
        in_hbm(outer_momentum),
    )
    weights, first, second, base_next, momentum_next = pl.pallas_call(
        placing_kernel,
        name="heads_in_place",
        out_shape=(
            jax.ShapeDtypeStruct((rows, width), F32),
            jax.ShapeDtypeStruct((rows, width), BF16),
            jax.ShapeDtypeStruct((rows, width), BF16),
            jax.ShapeDtypeStruct((share, columns), F32),
            jax.ShapeDtypeStruct((share, columns), F32),
        ),
        in_specs=[anywhere, smem] + [anywhere] * 5,
        out_specs=(anywhere,) * 5,
        scratch_shapes=[
            pltpu.SMEM((KVH,), jnp.int32),
            dma,
            dma((4, KVH)),
        ],
        compiler_params=pltpu.CompilerParams(vmem_limit_bytes=4 * 2**20),
    )(
        in_hbm(head_order),
        step_fragment,
        *(pltpu.with_memory_space_constraint(x, pltpu.VMEM) for x in made),
    )
    return (weights[None], first[None], second[None], base_next, momentum_next)


def solution(mesh):
    placed = (
        P("island", "fsdp", None),
        P("island", "fsdp", None),
        P("island", "fsdp", None),
        P("island", "fsdp", None),
        P("island", "fsdp", None),
        P(("fsdp", "island"), None),
        P(("fsdp", "island"), None),
        P(),
        P(),
    )
    return jax.shard_map(
        shards,
        mesh=mesh,
        in_specs=placed,
        out_specs=(
            P("island", "fsdp", None),
            P("island", "fsdp", None),
            P("island", "fsdp", None),
            P(("fsdp", "island"), None),
            P(("fsdp", "island"), None),
        ),
        check_vma=False,
    )
```

```python
import functools

import jax
import jax.numpy as jnp
from jax import lax
from jax.experimental import pallas as pl
from jax.experimental.pallas import tpu as pltpu
from jax.sharding import PartitionSpec as P

KVH = 8
HD = 128
SYNC = 4
Z = 8
HALF = 256
EIGHTH = 128
GC = 256
MESH = pl.DeviceIdType.MESH
F32 = jnp.float32
BF16 = jnp.bfloat16


def partial_product(a, b):
    return lax.dot_general(a, b, (((0,), (0,)), ((), ())), preferred_element_type=F32)


def sync_kernel(
    order,
    step_ref,
    tokens,
    cotangent,
    params,
    first_moment,
    second_moment,
    base,
    outer_momentum,
    new_weights,
    new_first,
    new_second,
    base_new,
    outer_new,
    order_ref,
    cot_raw,
    cot,
    tok,
    tok_stage,
    sent,
    got,
    side_sent,
    side_got,
    side_all,
    weights_v,
    first_v,
    second_v,
    base_v,
    outer_v,
    weights_p,
    first_p,
    second_p,
    frag,
    frag_got,
    base_sent,
    base_all,
    plan_load,
    cot_load,
    own_load,
    stage_load,
    state_load,
    y_send_cot,
    y_recv_cot,
    y_send_tok,
    y_recv_tok,
    z_send,
    z_recv,
    side_send,
    side_recv,
    cross_send,
    cross_recv,
    frag_send,
    frag_recv,
    base_send,
    base_recv,
):
    island = lax.axis_index("island")
    fsdp = lax.axis_index("fsdp")
    islands = lax.axis_size("island")
    z = fsdp // 2
    h = fsdp % 2
    partner = (island, z * 2 + (1 - h))
    up = (island, ((z + 1) % Z) * 2 + h)
    down = (island, ((z + Z - 1) % Z) * 2 + h)
    deltas = (4, 3, 5, 2, 6, 1, 7, 0)
    token_order = tuple((s, r) for pair in ((0,), (1, 2), (3, 4), (5, 6), (7,)) for r in range(2) for s in pair)

    cot_copy = pltpu.make_async_copy(cotangent, cot_raw, cot_load)

    def own_copy(s, r):
        column = ((z + deltas[s]) % Z * 2 + h) * 2 * HALF + r * HALF
        return pltpu.make_async_copy(
            tokens.at[:, pl.ds(pl.multiple_of(column, HALF), HALF)],
            tok.at[s, r, pl.ds(0, HALF), :],
            own_load.at[s, r],
        )

    def stage_copy(s, r):
        column = ((z + deltas[s]) % Z * 2 + (1 - h)) * 2 * HALF + r * HALF
        return pltpu.make_async_copy(
            tokens.at[:, pl.ds(pl.multiple_of(column, HALF), HALF)],
            tok_stage.at[s, r],
            stage_load.at[s, r],
        )

    def y_cot(g):
        return pltpu.make_async_remote_copy(
            cot.at[g, pl.ds(0, HALF), :],
            cot.at[g, pl.ds(HALF, HALF), :],
            y_send_cot.at[g],
            y_recv_cot.at[g],
            device_id=partner,
            device_id_type=MESH,
        )

    def y_tok(s, r, q=0, size=HALF):
        part = pl.ds(q * EIGHTH, size)
        return pltpu.make_async_remote_copy(
            tok_stage.at[s, r, :, part],
            tok.at[s, r, pl.ds(HALF, HALF), part],
            y_send_tok.at[s, r, q],
            y_recv_tok.at[s, r, q],
            device_id=partner,
            device_id_type=MESH,
        )

    plan = pltpu.make_async_copy(order, order_ref, plan_load)
    plan.start()
    cot_copy.start()
    for s, r in token_order[:2]:
        stage_copy(s, r).start()
    barrier = pltpu.get_barrier_semaphore()
    for peer in (partner, up, down):
        pl.semaphore_signal(barrier, inc=1, device_id=peer, device_id_type=MESH)

    def greet(k, carry):
        pl.semaphore_signal(
            barrier, inc=1, device_id=(lax.rem(island + k, islands), fsdp), device_id_type=MESH
        )
        return carry

    lax.fori_loop(1, islands, greet, 0)
    for s, r in token_order[2:6]:
        stage_copy(s, r).start()
    for s, r in token_order[:2]:
        own_copy(s, r).start()

    plan.wait()
    first_part = step_ref[0] == 0

    def head_of(j):
        return jnp.where(first_part, order_ref[j], order_ref[lax.rem(j + SYNC, KVH)])

    def columns_of(head, source, rows):
        found = source[rows, 0:HD]
        for other in range(1, KVH):
            found = lax.select(head == other, source[rows, other * HD : (other + 1) * HD], found)
        return found

    def side_copy(way, r):
        return pltpu.make_async_remote_copy(
            side_sent.at[r, pl.ds(way * EIGHTH, EIGHTH), :],
            side_got.at[way, r],
            side_send.at[way, r],
            side_recv.at[way, r],
            device_id=(up, down)[way],
            device_id_type=MESH,
        )

    def cross_copy(way, r):
        return pltpu.make_async_remote_copy(
            side_got.at[way, r],
            side_all.at[way, r],
            cross_send.at[way, r],
            cross_recv.at[way, r],
            device_id=partner,
            device_id_type=MESH,
        )

    def leaf_copy(way, g, r):
        rows = pl.ds(way * EIGHTH, EIGHTH)
        return pltpu.make_async_remote_copy(
            sent.at[0, 0, g, r, rows, :],
            got.at[way, 0, g, r, rows, :],
            z_send.at[way, 0, g, r],
            z_recv.at[way, 0, g, r],
            device_id=(up, down)[way],
            device_id_type=MESH,
        )

    def early_ends(g):
        for r in range(2):
            own_copy(0, r).wait()
            mine = cot[g, 0:HALF, :]
            sent[0, 0, g, r] = partial_product(tok[0, r, 0:HALF, :], mine).astype(BF16)
            for way in range(2):
                leaf_copy(way, g, r).start()
            side_sent[r] = partial_product(tok_stage[0, r], mine).astype(BF16)
            for way in range(2):
                side_copy(way, r).start()

    def sort_cot(g):
        for j in (2 * g, 2 * g + 1):
            cot[g, 0:HALF, (j % 2) * HD : (j % 2 + 1) * HD] = columns_of(
                head_of(j), cot_raw, slice(0, HALF)
            )

    def send_tok(s, r):
        stage_copy(s, r).wait()
        y_tok(s, r).start()

    cot_copy.wait()
    sort_cot(0)
    pl.semaphore_wait(barrier, 3 + islands - 1)
    send_tok(0, 0)
    y_cot(0).start()
    send_tok(0, 1)
    sort_cot(1)
    y_cot(1).start()
    sort_cot(3)
    early_ends(3)
    for s, r in token_order[2:6]:
        own_copy(s, r).start()
    for s, r in token_order[6:]:
        stage_copy(s, r).start()
    sort_cot(2)
    for r in range(2):
        for s in (1, 2):
            stage_copy(s, r).wait()
        for q in range(2):
            for s in (1, 2):
                y_tok(s, r, q, EIGHTH).start()
            if r != q:
                y_cot(2 + r).start()
    for s, r in token_order[6:]:
        own_copy(s, r).start()
    for s, r in token_order[6:14]:
        send_tok(s, r)
    state = [
        pltpu.make_async_copy(src, dst, state_load.at[i])
        for i, (src, dst) in enumerate(
            (
                (params, weights_v),
                (first_moment, first_v),
                (second_moment, second_v),
                (base, base_v),
                (outer_momentum, outer_v),
            )
        )
    ]
    for copy in state:
        copy.start()

    def z_copy(way, stage, g, r, low=0, size=HALF):
        rows = pl.ds(low, size)
        return pltpu.make_async_remote_copy(
            sent.at[way, stage, g, r, rows, :],
            got.at[way, stage, g, r, rows, :],
            z_send.at[way, stage, g, r],
            z_recv.at[way, stage, g, r],
            device_id=(up, down)[way],
            device_id_type=MESH,
        )

    def need_tok(s, r):
        own_copy(s, r).wait()
        y_tok(s, r).wait_recv()

    def need_cot(g):
        y_cot(g).wait_recv()

    def term(s, g, r):
        return partial_product(tok[s, r], cot[g])

    def pass_on(way, stage, s, g, r):
        total = term(s, g, r)
        z_copy(way, stage - 1, g, r).wait_recv()
        total = total + got[way, stage - 1, g, r].astype(F32)
        sent[way, stage, g, r] = total.astype(BF16)
        z_copy(way, stage, g, r).start()

    def ends(g, r):
        sent[0, 0, g, r] = term(0, g, r).astype(BF16)
        for way in range(2):
            leaf_copy(way, g, r).start()

    def third_half(way, q, g, r, early):
        rows = slice(q * EIGHTH, (q + 1) * EIGHTH)
        total = partial_product(tok[1 + way, r, :, rows], cot[g])
        if q == way:
            z_copy(way, 0, g, r, q * EIGHTH, EIGHTH).wait_recv()
            total = total + got[way, 0, g, r, rows, :].astype(F32)
            if early:
                cross_copy(way, r).wait_recv()
                total = total + side_all[way, r].astype(F32)
        sent[way, 1, g, r, rows, :] = total.astype(BF16)
        if not early:
            z_copy(way, 1, g, r, q * EIGHTH, EIGHTH).start()

    def third(q, r, low, count, early=False):
        def body(g, carry):
            for way in range(2):
                third_half(way, q, g, r, early)
            return carry

        lax.fori_loop(low, low + count, body, 0)

    def middle_first(stage):
        s_up, s_down = 2 * stage - 1, 2 * stage
        for r in range(2):
            need_tok(s_up, r)
            need_tok(s_down, r)

            def body(g, carry, r=r):
                pass_on(0, stage, s_up, g, r)
                pass_on(1, stage, s_down, g, r)
                return carry

            lax.fori_loop(0, 2, body, 0)

    def joined(way, stage, g):
        return pltpu.make_async_remote_copy(
            sent.at[way, stage, g],
            got.at[way, stage, g],
            z_send.at[way, stage, g, 0],
            z_recv.at[way, stage, g, 0],
            device_id=(up, down)[way],
            device_id_type=MESH,
        )

    def second(g, came_joined):
        for way in range(2):
            if came_joined:
                joined(way, 1, g).wait_recv()

            def body(r, carry, way=way):
                total = term(3 + way, g, r)
                if not came_joined:
                    z_copy(way, 1, g, r).wait_recv()
                sent[way, 2, g, r] = (total + got[way, 1, g, r].astype(F32)).astype(BF16)
                return carry

            lax.fori_loop(0, 2, body, 0)
            joined(way, 2, g).start()

    def last(g):
        for way in range(2):
            joined(way, 2, g).wait_recv()

        def body(r, carry):
            for way in range(2):
                total = term(5 + way, g, r) + got[way, 2, g, r].astype(F32)
                sent[way, 3, g, r] = total.astype(BF16)
                z_copy(way, 3, g, r).start()
            return carry

        lax.fori_loop(0, 2, body, 0)

    def sort_heads(low):
        def body(item, carry):
            j = low + item // 2
            rows = pl.ds(pl.multiple_of(item % 2 * HALF, HALF), HALF)
            head = head_of(j)
            weights_p[j, rows, :] = columns_of(head, weights_v, rows)
            first_p[j, rows, :] = columns_of(head, first_v, rows)
            second_p[j, rows, :] = columns_of(head, second_v, rows)
            return carry

        lax.fori_loop(0, 2 * SYNC, body, 0)

    def own_rows(low, fragment, first_item, last_item):
        def body(item, carry):
            r = item % 2
            g = low + item // 2
            rows = pl.ds(pl.multiple_of(r * HALF, HALF), HALF)
            grad = term(7, g, r)
            for way in range(2):
                z_copy(way, 3, g, r).wait_recv()
                grad = grad + got[way, 3, g, r].astype(F32)
            for k in range(2):
                j = 2 * g + k
                part = grad[:, k * HD : (k + 1) * HD]
                one = 0.9 * first_p[j, rows, :].astype(F32) + 0.1 * part
                two = 0.95 * second_p[j, rows, :].astype(F32) + 0.05 * part * part
                weights = weights_p[j, rows, :]
                stepped = weights - 0.01 * (one / (jnp.sqrt(two) + 1e-08) + 0.1 * weights)
                new_first[j, rows, :] = one.astype(BF16)
                new_second[j, rows, :] = two.astype(BF16)
                if fragment:
                    frag[rows, pl.ds(pl.multiple_of(j * HD, HD), HD)] = stepped.astype(BF16)
                else:
                    new_weights[j, rows, :] = stepped
            return carry

        lax.fori_loop(first_item, last_item, body, 0)

    share = base.shape[0]

    def frag_copy(k):
        peer = lax.rem(island + k, islands)
        return pltpu.make_async_remote_copy(
            frag.at[pl.ds(pl.multiple_of(peer * share, share), share), :],
            frag_got.at[k],
            frag_send.at[k],
            frag_recv.at[k],
            device_id=(peer, fsdp),
            device_id_type=MESH,
        )

    def base_copy(k):
        return pltpu.make_async_remote_copy(
            base_sent,
            base_all.at[pl.ds(pl.multiple_of(island * share, share), share), :],
            base_send.at[k],
            base_recv.at[k],
            device_id=(lax.rem(island + k, islands), fsdp),
            device_id_type=MESH,
        )

    def each_peer(action):
        def body(k, carry):
            action(k)
            return carry

        lax.fori_loop(1, islands, body, 0)

    def outer_step():
        mine = pl.ds(pl.multiple_of(island * share, share), share)

        def add(k, total):
            frag_copy(k).wait_recv()
            return total + frag_got[k].astype(F32)

        total = lax.fori_loop(1, islands, add, frag[mine, :].astype(F32))
        delta = base_v[...] - total / islands
        momentum = 0.9 * outer_v[...] + delta
        following = base_v[...] - 0.7 * (delta + 0.9 * momentum)
        base_sent[...] = following.astype(BF16)
        base_all[mine, :] = following.astype(BF16)
        base_new[...] = following
        outer_new[...] = momentum
        each_peer(lambda k: base_copy(k).start())

    need_cot(0)
    for r in range(2):
        y_tok(0, r).wait_recv()
        ends(0, r)
    need_cot(1)
    for r in range(2):
        ends(1, r)

    def need_third(q, r):
        for s in (1, 2):
            if q == 0:
                own_copy(s, r).wait()
            y_tok(s, r, q, EIGHTH).wait_recv()

    for q in range(2):
        need_third(q, 0)
        third(q, 0, 0, 2)
    for r in range(2):
        for way in range(2):
            side_copy(way, r).wait_recv()
            cross_copy(way, r).start()
    for r in range(2):
        send_tok(7, r)
    need_cot(2)
    for r in range(2):
        ends(2, r)
    for q in range(2):
        third(q, 0, 2, 1)
    for q in range(2):
        need_third(q, 1)
        third(q, 1, 0, 3)
    need_cot(3)
    for copy in state:
        copy.wait()
    sort_heads(0)
    middle_first(2)
    middle_first(3)
    for r in range(2):
        for q in range(2):
            third(q, r, 3, 1, True)
    for way in range(2):
        joined(way, 1, 3).start()
    second(2, False)
    sort_heads(SYNC)
    need_tok(7, 0)
    need_tok(7, 1)
    own_rows(0, True, 0, 4)
    each_peer(lambda k: frag_copy(k).start())
    second(3, True)
    last(2)
    outer_step()
    last(3)
    own_rows(2, False, 0, 2)
    each_peer(lambda k: base_copy(k).wait_recv())
    for j in range(SYNC):
        new_weights[j] = base_all[:, j * HD : (j + 1) * HD].astype(F32)
    own_rows(2, False, 2, 4)

    for g in range(4):
        y_cot(g).wait_send()
    for s, r in token_order:
        if s in (1, 2):
            for q in range(2):
                y_tok(s, r, q, EIGHTH).wait_send()
        else:
            y_tok(s, r).wait_send()

    for r in range(2):
        for way in range(2):
            side_copy(way, r).wait_send()
            cross_copy(way, r).wait_send()

    def leaf_sends(item, carry):
        for way in range(2):
            z_copy(way, 0, item // 2, item % 2, way * EIGHTH, EIGHTH).wait_send()
        return carry

    lax.fori_loop(0, 8, leaf_sends, 0)

    def sends(item, carry):
        r = item % 2
        for way in range(2):
            for stage, groups in ((1, (0, 1, 2)), (2, (0, 1)), (3, (0, 1, 2, 3))):
                for g in groups:
                    z_copy(way, stage, g, r).wait_send()
        return carry

    lax.fori_loop(0, 2, sends, 0)
    for way in range(2):
        for stage, g in ((1, 3), (2, 2), (2, 3)):
            joined(way, stage, g).wait_send()
    each_peer(lambda k: frag_copy(k).wait_send())
    each_peer(lambda k: base_copy(k).wait_send())


def placing_kernel(
    order,
    step_ref,
    weights,
    first,
    second,
    base,
    momentum,
    w_out,
    f_out,
    s_out,
    b_out,
    m_out,
    order_ref,
    plan_load,
    sems,
):
    plan = pltpu.make_async_copy(order, order_ref, plan_load)
    plan.start()
    copies = []
    for i, (source, out) in enumerate(((base, b_out), (momentum, m_out))):
        copies.append(pltpu.make_async_copy(source, out, sems.at[3, i]))
        copies[-1].start()
    plan.wait()
    for head in range(KVH):
        place = 0
        for j in range(1, KVH):
            found = order_ref[lax.rem(step_ref[0] * SYNC + j, KVH)] == head
            place = place + jnp.where(found, j, 0)
        columns = pl.ds(head * HD, HD)
        for i, (source, out) in enumerate(((weights, w_out), (first, f_out), (second, s_out))):
            copies.append(
                pltpu.make_async_copy(source.at[place], out.at[:, columns], sems.at[i, head])
            )
            copies[-1].start()
    for copy in copies:
        copy.wait()


def shards(
    tokens,
    cotangent,
    params,
    first_moment,
    second_moment,
    base,
    outer_momentum,
    head_order,
    step_fragment,
):
    rows, width = params.shape[1:]
    share, columns = base.shape
    islands = lax.axis_size("island")
    smem = pl.BlockSpec(memory_space=pltpu.SMEM)
    anywhere = pl.BlockSpec(memory_space=pl.ANY)
    dma = pltpu.SemaphoreType.DMA

    def in_hbm(x):
        return pltpu.with_memory_space_constraint(x, pltpu.HBM)

    made = pl.pallas_call(
        sync_kernel,
        name="inner_step_and_outer_sync",
        out_shape=(
            pltpu.VMEM((KVH, rows, HD), F32),
            pltpu.VMEM((KVH, rows, HD), BF16),
            pltpu.VMEM((KVH, rows, HD), BF16),
            pltpu.VMEM((share, columns), F32),
            pltpu.VMEM((share, columns), F32),
        ),
        in_specs=[anywhere, smem] + [anywhere] * 7,
        out_specs=(pl.BlockSpec(memory_space=pltpu.VMEM),) * 5,
        scratch_shapes=[
            pltpu.SMEM((KVH,), jnp.int32),
            pltpu.VMEM((HALF, width), BF16),
            pltpu.VMEM((4, 2 * HALF, GC), BF16),
            pltpu.VMEM((Z, 2, 2 * HALF, HALF), BF16),
            pltpu.VMEM((Z, 2, HALF, HALF), BF16),
            pltpu.VMEM((2, 4, 4, 2, HALF, GC), BF16),
            pltpu.VMEM((2, 4, 4, 2, HALF, GC), BF16),
            pltpu.VMEM((2, HALF, GC), BF16),
            pltpu.VMEM((2, 2, EIGHTH, GC), BF16),
            pltpu.VMEM((2, 2, EIGHTH, GC), BF16),
            pltpu.VMEM((rows, width), F32),
            pltpu.VMEM((rows, width), BF16),
            pltpu.VMEM((rows, width), BF16),
            pltpu.VMEM((share, columns), F32),
            pltpu.VMEM((share, columns), F32),
            pltpu.VMEM((KVH, rows, HD), F32),
            pltpu.VMEM((KVH, rows, HD), BF16),
            pltpu.VMEM((KVH, rows, HD), BF16),
            pltpu.VMEM((rows, columns), BF16),
            pltpu.VMEM((16, share, columns), BF16),
            pltpu.VMEM((share, columns), BF16),
            pltpu.VMEM((rows, columns), BF16),
            dma,
            dma,
            dma((Z, 2)),
            dma((Z, 2)),
            dma((5,)),
            dma((4,)),
            dma((4,)),
            dma((Z, 2, 2)),
            dma((Z, 2, 2)),
            dma((2, 4, 4, 2)),
            dma((2, 4, 4, 2)),
            dma((2, 2)),
            dma((2, 2)),
            dma((2, 2)),
            dma((2, 2)),
            dma((16,)),
            dma((16,)),
            dma((16,)),
            dma((16,)),
        ],
        compiler_params=pltpu.CompilerParams(
            collective_id=0, has_side_effects=True, vmem_limit_bytes=48 * 2**20
        ),
        cost_estimate=pl.CostEstimate(
            flops=2 * 256 * 8192 * 1024, bytes_accessed=13 * 2**20, transcendentals=rows * width
        ),
    )(
        in_hbm(head_order),
        step_fragment,
        in_hbm(tokens[0]),
        in_hbm(cotangent[0]),
        in_hbm(params[0]),
        in_hbm(first_moment[0]),
        in_hbm(second_moment[0]),
        in_hbm(base),
        in_hbm(outer_momentum),
    )
    weights, first, second, base_next, momentum_next = pl.pallas_call(
        placing_kernel,
        name="heads_in_place",
        out_shape=(
            jax.ShapeDtypeStruct((rows, width), F32),
            jax.ShapeDtypeStruct((rows, width), BF16),
            jax.ShapeDtypeStruct((rows, width), BF16),
            jax.ShapeDtypeStruct((share, columns), F32),
            jax.ShapeDtypeStruct((share, columns), F32),
        ),
        in_specs=[anywhere, smem] + [anywhere] * 5,
        out_specs=(anywhere,) * 5,
        scratch_shapes=[
            pltpu.SMEM((KVH,), jnp.int32),
            dma,
            dma((4, KVH)),
        ],
        compiler_params=pltpu.CompilerParams(vmem_limit_bytes=4 * 2**20),
    )(
        in_hbm(head_order),
        step_fragment,
        *(pltpu.with_memory_space_constraint(x, pltpu.VMEM) for x in made),
    )
    return (weights[None], first[None], second[None], base_next, momentum_next)


def solution(mesh):
    placed = (
        P("island", "fsdp", None),
        P("island", "fsdp", None),
        P("island", "fsdp", None),
        P("island", "fsdp", None),
        P("island", "fsdp", None),
        P(("fsdp", "island"), None),
        P(("fsdp", "island"), None),
        P(),
        P(),
    )
    return jax.shard_map(
        shards,
        mesh=mesh,
        in_specs=placed,
        out_specs=(
            P("island", "fsdp", None),
            P("island", "fsdp", None),
            P("island", "fsdp", None),
            P(("fsdp", "island"), None),
            P(("fsdp", "island"), None),
        ),
        check_vma=False,
    )
```
